32 devices in a mesh: row: 8 (over y, x, core), col: 4 (over z).
Axes of the slice: x: 2, y: 2, z: 4, core: 2. Of those that a mesh axis runs over, the one named last changes fastest.
Arguments:
- blocks: float32 [8, 4, 4, 8, 2, 64, 128], P('row', 'col'), may hold values from 0.5 to 1620
- plan: int32 [8, 4, 4, 8, 2], P('row', 'col'), may hold values from 0 to 511, as said below
- live: int32 [8, 4, 4, 8], P('row', 'col'), may hold values from 1 to 2, as said below
- row_emb: float32 [300, 8192], P(None, ('row', 'col')), may hold values from -1.5 to 1.5
- col_emb: float32 [300, 16384], P(None, ('col', 'row')), may hold values from -1.5 to 1.5
- row_acc: float32 [300, 8192], P(None, ('row', 'col')), may hold values from 0.5 to 5
- col_acc: float32 [300, 16384], P(None, ('col', 'row')), may hold values from 0.5 to 5
Outputs:
- new_row_emb: float32 [300, 8192], P(None, ('row', 'col'))
- new_col_emb: float32 [300, 16384], P(None, ('col', 'row'))
- new_row_acc: float32 [300, 8192], P(None, ('row', 'col'))
- new_col_acc: float32 [300, 16384], P(None, ('col', 'row'))
The draws below stay inside these ranges and needn't reach their ends.
Inputs may be any that keep to these rules, and one draw needn't show every extreme that they name: plan[r, c, c2, r2, p] is a sub-block number of tile (r, c); numbers may repeat and repeated slots add. Over all index pairs (r2, c2), slot 0 names every sub-block row and every sub-block column of each tile. Slots at or past live[r, c, c2, r2] hold values that are not counts. In every draw some tile gets 2 live slots from every index pair.
All inputs are finite; a program needn't handle non-finite values.
Results may differ from the reference program's by a relative error of at most 0.0003.
Values sent between devices are 32-bit elements; how exact they have to be, the bound alone decides.
A program may use at most 192 MiB of HBM per device.

```python
import math
import jax
import jax.numpy as jnp
from jax import lax

DIM = 300
TILE_WORD_ROWS = 1024
TILE_WORD_COLUMNS = 4096
SUBBLOCK_COLUMNS = 128
SUBBLOCK_ROWS = 64
SLOTS_PER_DEVICE = 2
ROWS = 8192
COLS = 16384
N_ROW = 8
N_COL = 4


def draw_blocks(key, part):
    complete_shape = (N_ROW, N_COL, N_COL, N_ROW, SLOTS_PER_DEVICE, SUBBLOCK_ROWS, SUBBLOCK_COLUMNS)
    col_rise = 1.0 + 2.0 * lax.broadcasted_iota(jnp.float32, complete_shape, 2) / max(N_COL - 1, 1)
    row_rise = 1.0 + 2.0 * lax.broadcasted_iota(jnp.float32, complete_shape, 3) / max(N_ROW - 1, 1)
    subkey = jax.random.fold_in(key, 5)
    values = jnp.exp(jax.random.uniform(subkey, complete_shape, jnp.float32, math.log(0.5), math.log(20.0)))
    return values * col_rise * row_rise


def draw_plan(key, part):
    complete_shape = (N_ROW, N_COL, N_COL, N_ROW, SLOTS_PER_DEVICE)
    grid_row_count = TILE_WORD_ROWS // SUBBLOCK_ROWS
    grid_column_count = TILE_WORD_COLUMNS // SUBBLOCK_COLUMNS
    owners = N_ROW * N_COL
    key_any, key_rows, key_cols = jax.random.split(jax.random.fold_in(key, 11), 3)
    anywhere = jax.random.randint(key_any, complete_shape, 0, grid_row_count * grid_column_count, dtype=jnp.int32)
    rows_perm = jax.vmap(lambda subkey: jax.random.permutation(subkey, owners))(jax.random.split(key_rows, owners))
    cols_perm = jax.vmap(lambda subkey: jax.random.permutation(subkey, owners))(jax.random.split(key_cols, owners))
    first_slot = (rows_perm % grid_row_count * grid_column_count + cols_perm % grid_column_count).astype(jnp.int32)
    first_slot = first_slot.reshape(N_ROW, N_COL, N_COL, N_ROW)
    return jnp.concatenate([first_slot[..., None], anywhere[..., 1:]], axis=-1)


def draw_live(key, part):
    complete_shape = (N_ROW, N_COL, N_COL, N_ROW)
    key_base, key_pick = jax.random.split(jax.random.fold_in(key, 23))
    counts_base = jax.random.randint(key_base, complete_shape, 1, SLOTS_PER_DEVICE + 1, dtype=jnp.int32)
    chosen = jax.random.randint(key_pick, (), 0, N_ROW * N_COL, dtype=jnp.int32)
    owner_ids = lax.broadcasted_iota(jnp.int32, complete_shape, 0) * N_COL + lax.broadcasted_iota(jnp.int32, complete_shape, 1)
    return jnp.where(owner_ids == chosen, SLOTS_PER_DEVICE, counts_base).astype(jnp.int32)


def shard_levels(own_key, dims, cuts, smallest, top_value):
    def one(position, blocks):
        draws = jax.random.uniform(jax.random.fold_in(jax.random.fold_in(own_key, 6), position), (blocks,), jnp.float32, smallest / len(cuts), top_value / len(cuts))
        return jnp.repeat(jnp.exp(draws), dims[position] // blocks).reshape((-1,) + (1,) * (len(dims) - position - 1))

    loudness = one(*cuts[0])
    for cut in cuts[1:]:
        loudness = loudness * one(*cut)
    return loudness


def noise(own_key, shape, scale, reach, pieces=(), held_as=jnp.bfloat16):
    drawn = scale * jax.random.normal(own_key, shape, jnp.float32)
    if pieces:
        drawn = drawn * shard_levels(own_key, shape, pieces, -0.22, 0.18)
    return jnp.clip(drawn, -reach, reach).astype(held_as)


def setup_inputs(seed: int = 0) -> dict:
    splits = jax.random.split(jax.random.key(seed), 8)
    return {
        "blocks": draw_blocks(jax.random.fold_in(splits[7], 71), 0),
        "plan": draw_plan(jax.random.fold_in(splits[7], 71), 0),
        "live": draw_live(jax.random.fold_in(splits[7], 71), 0),
        "row_emb": noise(splits[3], (DIM, ROWS), 0.25, 1.5, ((1, 32),), jnp.float32),
        "col_emb": noise(splits[4], (DIM, COLS), 0.25, 1.5, ((1, 32),), jnp.float32),
        "row_acc": jnp.clip(jnp.exp(math.log(5.0) - 2.3025851 * jax.random.uniform(splits[5], (DIM, ROWS), jnp.float32) ** shard_levels(splits[5], (DIM, ROWS), ((1, 32),), -0.2, 0.2)), 0.5, 5.0),
        "col_acc": jnp.clip(jnp.exp(math.log(5.0) - 2.3025851 * jax.random.uniform(splits[6], (DIM, COLS), jnp.float32) ** shard_levels(splits[6], (DIM, COLS), ((1, 32),), -0.2, 0.2)), 0.5, 5.0),
    }


LEARNING_RATE = 0.2

def owner_tile(blocks, plan, live, row_index, col_index):
    slot_entries = jnp.swapaxes(blocks[:, :, col_index, row_index], 0, 1)
    places = plan[row_index, col_index]
    limits = live[row_index, col_index]
    slot_ids = lax.broadcasted_iota(jnp.int32, places.shape, 2)
    grid_row_count = TILE_WORD_ROWS // SUBBLOCK_ROWS
    grid_column_count = TILE_WORD_COLUMNS // SUBBLOCK_COLUMNS
    block_total = grid_row_count * grid_column_count
    target = jnp.where(slot_ids < limits[:, :, None], places, block_total).astype(jnp.int32)
    flat_layout = slot_entries.reshape(-1, SUBBLOCK_ROWS * SUBBLOCK_COLUMNS)
    dense_block_matrix = jax.ops.segment_sum(flat_layout, target.reshape(-1), num_segments=block_total + 1)[:block_total]
    return dense_block_matrix.reshape(grid_row_count, grid_column_count, SUBBLOCK_ROWS, SUBBLOCK_COLUMNS).transpose(0, 2, 1, 3).reshape(TILE_WORD_ROWS, TILE_WORD_COLUMNS)

def reference(blocks, plan, live, row_emb, col_emb, row_acc, col_acc):
    tile_ids = jnp.arange(N_ROW * N_COL, dtype=jnp.int32)
    highest = lax.Precision.HIGHEST

    def partial_sums(tile_id):
        tile_counts = owner_tile(blocks, plan, live, tile_id // N_COL, tile_id % N_COL)
        return (lax.optimization_barrier(jnp.sum(tile_counts, axis=1)), lax.optimization_barrier(jnp.sum(tile_counts, axis=0)))
    row_parts, col_parts = lax.map(partial_sums, tile_ids)
    row_mass = lax.optimization_barrier(jnp.sum(row_parts.reshape(N_ROW, N_COL, TILE_WORD_ROWS), axis=1))
    col_mass = lax.optimization_barrier(jnp.sum(col_parts.reshape(N_ROW, N_COL, TILE_WORD_COLUMNS), axis=0))
    grand_total = jnp.sum(row_mass)
    loss_scale = 4.0 * float(ROWS * COLS) ** (-0.25)

    def accumulate(totals, tile_id):
        row_grad, col_grad = totals
        row_index = tile_id // N_COL
        col_index = tile_id % N_COL
        tile_counts = owner_tile(blocks, plan, live, row_index, col_index)
        row_block = lax.dynamic_slice_in_dim(row_emb, row_index * TILE_WORD_ROWS, TILE_WORD_ROWS, 1)
        col_block = lax.dynamic_slice_in_dim(col_emb, col_index * TILE_WORD_COLUMNS, TILE_WORD_COLUMNS, 1)
        scores = jnp.dot(row_block.T, col_block, precision=highest)
        baseline = jnp.log(grand_total) - jnp.log(row_mass[row_index])[:, None] - jnp.log(col_mass[col_index])[None, :]
        positive = tile_counts > 0
        pmi_target = jnp.log(jnp.where(positive, tile_counts, 1.0)) + baseline
        confidence = 0.1 + 0.25 * jnp.sqrt(tile_counts)
        loss_grad = jnp.where(positive, confidence * (scores - pmi_target), jax.nn.sigmoid(scores - baseline)) * loss_scale
        row_term = jnp.dot(col_block, loss_grad.T, precision=highest)
        col_term = jnp.dot(row_block, loss_grad, precision=highest)
        row_old = lax.dynamic_slice_in_dim(row_grad, row_index * TILE_WORD_ROWS, TILE_WORD_ROWS, 1)
        col_old = lax.dynamic_slice_in_dim(col_grad, col_index * TILE_WORD_COLUMNS, TILE_WORD_COLUMNS, 1)
        row_grad = lax.dynamic_update_slice_in_dim(row_grad, row_old + row_term, row_index * TILE_WORD_ROWS, 1)
        col_grad = lax.dynamic_update_slice_in_dim(col_grad, col_old + col_term, col_index * TILE_WORD_COLUMNS, 1)
        return ((row_grad, col_grad), None)
    start = (jnp.zeros((DIM, ROWS), jnp.float32), jnp.zeros((DIM, COLS), jnp.float32))
    (row_grad, col_grad), _ = lax.scan(accumulate, start, tile_ids)
    new_row_acc = row_acc + row_grad * row_grad
    new_col_acc = col_acc + col_grad * col_grad
    new_row_emb = row_emb - LEARNING_RATE * row_grad / jnp.sqrt(new_row_acc)
    new_col_emb = col_emb - LEARNING_RATE * col_grad / jnp.sqrt(new_col_acc)
    return (new_row_emb, new_col_emb, new_row_acc, new_col_acc)
```

```python
import functools

import jax
import jax.numpy as jnp
from jax import lax
from jax.experimental import pallas as pl
from jax.experimental.pallas import tpu as pltpu
from jax.sharding import PartitionSpec as P

LEARNING_RATE = 0.2
MESH = pl.DeviceIdType.MESH
VMEM_LIMIT = 56 * 1024 * 1024


def round_up(value, step):
    return -(-value // step) * step


def remote(src, dst, send_sem, recv_sem, device):
    return pltpu.make_async_remote_copy(
        src_ref=src, dst_ref=dst, send_sem=send_sem, recv_sem=recv_sem,
        device_id=device, device_id_type=MESH,
    )


def exchange_kernel(
    n_row, n_col, blocks, row_emb, col_emb, arrived, rows, cols,
    a_send, a_recv, r_send, r_recv, c_send, c_recv, f_send, f_recv, local_sem,
):
    r = lax.axis_index("row")
    c = lax.axis_index("col")
    core = lax.rem(r, 2)
    sibling = r + 1 - 2 * core
    chips = n_row // 2
    total = n_row * n_col

    def peer(k):
        return lax.rem(r + k % n_row, n_row), lax.rem(c + k // n_row, n_col)

    def chip_peer(t):
        return lax.rem(r + 2 * t, n_row)

    barrier = pltpu.get_barrier_semaphore()

    @pl.loop(1, total)
    def _(k):
        pl.semaphore_signal(barrier, inc=1, device_id=peer(k), device_id_type=MESH)

    pl.semaphore_wait(barrier, total - 1)

    local = [
        pltpu.make_async_copy(blocks.at[c, r], arrived.at[c, r], local_sem.at[0]),
        pltpu.make_async_copy(row_emb, rows.at[c], local_sem.at[1]),
        pltpu.make_async_copy(col_emb, cols.at[r], local_sem.at[2]),
    ]

    def row_copy(k):
        return remote(row_emb, rows.at[c], r_send.at[k], r_recv.at[k], (r, lax.rem(c + k, n_col)))

    def col_copy(t):
        return remote(col_emb, cols.at[r], c_send.at[t], c_recv.at[t], (chip_peer(t), c))

    def pair_copy():
        return remote(col_emb, cols.at[r], f_send.at[0], f_recv.at[0], (sibling, c))

    def forward(t):
        origin = lax.rem(r + n_row - 2 * t, n_row)
        return remote(cols.at[origin], cols.at[origin], f_send.at[t], f_recv.at[t], (sibling, c))

    def block_copy(k):
        pr, pc = peer(k)
        return remote(blocks.at[pc, pr], arrived.at[c, r], a_send.at[k], a_recv.at[k], (pr, pc))

    @pl.loop(1, chips)
    def _(t):
        col_copy(t).start()

    pair_copy().start()

    @pl.loop(1, total)
    def _(k):
        block_copy(total - k).start()

    @pl.loop(1, n_col)
    def _(k):
        row_copy(k).start()

    for copy in local:
        copy.start()

    @pl.loop(1, chips)
    def _(t):
        col_copy(t).wait_recv()
        forward(t).start()

    for copy in local:
        copy.wait()
    pair_copy().wait()

    @pl.loop(1, chips)
    def _(t):
        col_copy(t).wait_send()
        forward(t).wait()

    @pl.loop(1, n_col)
    def _(k):
        row_copy(k).wait()

    @pl.loop(1, total)
    def _(k):
        block_copy(k).wait()


def exchange(n_row, n_col, blocks, row_emb, col_emb):
    f32 = jnp.float32
    any_spec = pl.BlockSpec(memory_space=pl.ANY)
    dma = pltpu.SemaphoreType.DMA
    total = n_row * n_col
    return pl.pallas_call(
        functools.partial(exchange_kernel, n_row, n_col),
        out_shape=(
            jax.ShapeDtypeStruct(blocks.shape, f32),
            jax.ShapeDtypeStruct((n_col,) + row_emb.shape, f32),
            jax.ShapeDtypeStruct((n_row,) + col_emb.shape, f32),
        ),
        in_specs=[any_spec] * 3,
        out_specs=(any_spec,) * 3,
        scratch_shapes=[
            dma((total,)), dma((total,)), dma((n_col,)), dma((n_col,)),
            dma((n_row // 2,)), dma((n_row // 2,)), dma((n_row // 2,)), dma((n_row // 2,)), dma((3,)),
        ],
        compiler_params=pltpu.CompilerParams(collective_id=0, has_side_effects=True),
        name="exchange",
    )(blocks, row_emb, col_emb)


def merge_kernel(scale, plan, live, blocks, gain, offset, table, row_part, col_part, row_sum, seen):
    slots, sub_rows, sub_cols = blocks.shape
    places = table.shape[0]
    grid_columns = col_part.shape[0]

    @pl.loop(0, places)
    def _(b):
        table[b] = slots

    row_sum[...] = jnp.zeros_like(row_sum)
    col_part[...] = jnp.zeros_like(col_part)
    gain[slots] = jnp.zeros((sub_rows, sub_cols), jnp.float32)
    offset[slots] = jnp.zeros((sub_rows, sub_cols), jnp.float32)

    @pl.loop(0, slots)
    def _(k):
        @pl.when(live[k] > 0)
        def _():
            place = plan[k]
            i = place // grid_columns
            j = place - i * grid_columns
            block = blocks[k]
            row_sum[i] = row_sum[i] + block
            col_part[pl.ds(j, 1), :] += jnp.sum(block, axis=0, keepdims=True)
            first = table[place]
            fresh = first == slots
            target = jnp.where(fresh, k, first)
            table[place] = target

            @pl.when(fresh)
            def _():
                seen[k] = block

            @pl.when(jnp.logical_not(fresh))
            def _():
                seen[target] = seen[target] + block
                seen[k] = block

        @pl.when(live[k] <= 0)
        def _():
            seen[k] = jnp.ones((sub_rows, sub_cols), jnp.float32)

    @pl.loop(0, slots)
    def _(k):
        counts = seen[k]
        confidence = scale * (0.1 + 0.25 * jnp.sqrt(counts))
        gain[k] = confidence
        offset[k] = -confidence * jnp.log(counts)

    row_part[...] = jnp.sum(row_sum[...], axis=2)


def merge(scale, plan, live, blocks, grid_rows, grid_columns):
    slots, sub_rows, sub_cols = blocks.shape
    f32 = jnp.float32
    smem = pl.BlockSpec(memory_space=pltpu.SMEM)
    vmem = pl.BlockSpec(memory_space=pltpu.VMEM)
    return pl.pallas_call(
        functools.partial(merge_kernel, scale),
        out_shape=(
            jax.ShapeDtypeStruct((slots + 1, sub_rows, sub_cols), f32),
            jax.ShapeDtypeStruct((slots + 1, sub_rows, sub_cols), f32),
            jax.ShapeDtypeStruct((grid_rows * grid_columns,), jnp.int32),
            jax.ShapeDtypeStruct((grid_rows, sub_rows), f32),
            jax.ShapeDtypeStruct((grid_columns, sub_cols), f32),
        ),
        in_specs=[smem, smem, vmem],
        out_specs=(vmem, vmem, smem, vmem, vmem),
        scratch_shapes=[
            pltpu.VMEM((grid_rows, sub_rows, sub_cols), f32),
            pltpu.VMEM((slots, sub_rows, sub_cols), f32),
        ],
        compiler_params=pltpu.CompilerParams(vmem_limit_bytes=VMEM_LIMIT),
        name="merge",
    )(plan, live, blocks)


def mass_kernel(
    n_row, n_col, row_part, col_part, row_log, col_log, row_in, col_in, tot_out, tot_in,
    r_send, r_recv, c_send, c_recv, t_send, t_recv,
):
    r = lax.axis_index("row")
    c = lax.axis_index("col")

    def row_peer(k):
        return (lax.rem(r + k, n_row), c)

    def col_peer(k):
        return (r, lax.rem(c + k, n_col))

    barrier = pltpu.get_barrier_semaphore()

    @pl.loop(1, n_row)
    def _(k):
        pl.semaphore_signal(barrier, inc=1, device_id=row_peer(k), device_id_type=MESH)

    @pl.loop(1, n_col)
    def _(k):
        pl.semaphore_signal(barrier, inc=1, device_id=col_peer(k), device_id_type=MESH)

    pl.semaphore_wait(barrier, n_row + n_col - 2)

    def col_copy(k):
        return remote(col_part, col_in.at[k], c_send.at[k], c_recv.at[k], row_peer(k))

    def row_copy(k):
        return remote(row_part, row_in.at[k], r_send.at[k], r_recv.at[k], col_peer(k))

    def tot_copy(k):
        return remote(tot_out, tot_in.at[k], t_send.at[k], t_recv.at[k], col_peer(k))

    @pl.loop(1, n_row)
    def _(k):
        col_copy(k).start()

    @pl.loop(1, n_col)
    def _(k):
        row_copy(k).start()

    @pl.loop(1, n_row)
    def _(k):
        col_copy(k).wait()

    col_mass = col_part[...]
    for k in range(1, n_row):
        col_mass = col_mass + col_in[k]
    part = jnp.sum(jnp.sum(col_mass, axis=0, keepdims=True), axis=1, keepdims=True)
    tot_out[...] = jnp.broadcast_to(part, tot_out.shape)

    @pl.loop(1, n_col)
    def _(k):
        tot_copy(k).start()

    @pl.loop(1, n_col)
    def _(k):
        row_copy(k).wait()

    row_mass = row_part[...]
    for k in range(1, n_col):
        row_mass = row_mass + row_in[k]
    row_log[...] = jnp.log(row_mass)

    @pl.loop(1, n_col)
    def _(k):
        tot_copy(k).wait()

    grand = tot_out[...]
    for k in range(1, n_col):
        grand = grand + tot_in[k]
    col_log[...] = jnp.log(col_mass) - jnp.log(grand[0:1, :])


def masses(n_row, n_col, row_part, col_part):
    f32 = jnp.float32
    vmem = pl.BlockSpec(memory_space=pltpu.VMEM)
    dma = pltpu.SemaphoreType.DMA
    return pl.pallas_call(
        functools.partial(mass_kernel, n_row, n_col),
        out_shape=(
            jax.ShapeDtypeStruct(row_part.shape, f32),
            jax.ShapeDtypeStruct(col_part.shape, f32),
        ),
        in_specs=[vmem] * 2,
        out_specs=(vmem,) * 2,
        scratch_shapes=[
            pltpu.VMEM((n_col,) + row_part.shape, f32),
            pltpu.VMEM((n_row,) + col_part.shape, f32),
            pltpu.VMEM((8, col_part.shape[1]), f32),
            pltpu.VMEM((n_col, 8, col_part.shape[1]), f32),
            dma((n_col,)), dma((n_col,)), dma((n_row,)), dma((n_row,)), dma((n_col,)), dma((n_col,)),
        ],
        compiler_params=pltpu.CompilerParams(collective_id=1, has_side_effects=True),
        name="masses",
    )(row_part, col_part)


def gradient_kernel(
    n_row, n_col, dim, dim_pad, depth, half_scale,
    table, rows, cols, gain, offset, row_log, col_log, row_share, col_share,
    pad_row, pad_col, row_left, row_turned, col_right, lg_hi, lg_lo, row_sum, col_out, pair_in, chip_in, row_in,
    p_send, p_recv, h_send, h_recv, r_send, r_recv,
):
    f32 = jnp.float32
    bf16 = jnp.bfloat16
    r = lax.axis_index("row")
    c = lax.axis_index("col")
    core = lax.rem(r, 2)
    chip = r // 2
    chips = n_row // 2
    sibling = r + 1 - 2 * core
    row_width = rows.shape[2]
    col_width = cols.shape[2]
    sub_rows, sub_cols = gain.shape[1:]
    per_chunk = col_width // sub_cols
    grid_columns = col_log.shape[0]

    barrier = pltpu.get_barrier_semaphore()
    pl.semaphore_signal(barrier, inc=1, device_id=(sibling, c), device_id_type=MESH)

    @pl.loop(1, chips)
    def _(t):
        pl.semaphore_signal(barrier, inc=1, device_id=(lax.rem(r + 2 * t, n_row), c), device_id_type=MESH)

    @pl.loop(1, n_col)
    def _(k):
        pl.semaphore_signal(barrier, inc=1, device_id=(r, lax.rem(c + k, n_col)), device_id_type=MESH)

    pl.semaphore_wait(barrier, chips + n_col - 1)

    def pair_copy(t):
        return remote(col_out.at[2 * t], pair_in.at[t], p_send.at[t], p_recv.at[t], (sibling, c))

    def chip_copy(t):
        return remote(
            col_out.at[2 * t + 1], chip_in.at[t], h_send.at[t], h_recv.at[t],
            (lax.rem(r + 2 * (t + 1), n_row), c),
        )

    def row_copy(k):
        target = lax.rem(c + k, n_col)
        return remote(row_sum.at[target], row_in.at[k], r_send.at[k], r_recv.at[k], (r, target))

    pad_row[...] = jnp.zeros_like(pad_row)
    pad_col[...] = jnp.zeros_like(pad_col)
    row_left[...] = jnp.zeros_like(row_left)
    col_right[...] = jnp.zeros_like(col_right)
    row_sum[...] = jnp.zeros_like(row_sum)
    for q in range(n_col):
        pad_row[0:dim, :] = rows[q]
        value = pad_row[...]
        high = value.astype(bf16)
        low = (value - high.astype(f32)).astype(bf16)
        span = slice(q * row_width, (q + 1) * row_width)
        row_left[0:dim_pad, span] = high
        row_left[dim_pad : 2 * dim_pad, span] = low
        row_left[2 * dim_pad : 3 * dim_pad, span] = high
        row_turned[span, :] = row_left[:, span].T

    @pl.loop(0, 2 * chips)
    def _(step):
        t = step // 2
        second = step % 2
        chunk = 2 * lax.rem(chip + 1 + t, chips) + jnp.where(second == 1, core, 1 - core)
        pad_col[0:dim, :] = cols[chunk]
        value = pad_col[...]
        high = value.astype(bf16)
        low = (value - high.astype(f32)).astype(bf16)
        col_right[0:dim_pad, :] = high
        col_right[dim_pad : 2 * dim_pad, :] = high
        col_right[2 * dim_pad : 3 * dim_pad, :] = low

        @pl.loop(0, n_col)
        def _(q):
            base = pl.multiple_of(q * row_width, row_width)
            scores = jnp.dot(row_turned[pl.ds(base, row_width), :], col_right[...], preferred_element_type=f32)
            strips = []
            for j in range(per_chunk):
                column = chunk * per_chunk + j
                col_base = col_log[pl.ds(column, 1), :]
                pieces = []
                for i in range(row_width // sub_rows):
                    line = q * (row_width // sub_rows) + i
                    slot = table[line * grid_columns + column]
                    a = gain[slot]
                    b = offset[slot]
                    row_base = row_log[pl.ds(pl.multiple_of(line * sub_rows, sub_rows), sub_rows), :]
                    x = (
                        scores[i * sub_rows : (i + 1) * sub_rows, j * sub_cols : (j + 1) * sub_cols]
                        + row_base + col_base
                    )
                    pieces.append(jnp.where(a > 0, a * x + b, half_scale + half_scale * jnp.tanh(0.5 * x)))
                strips.append(jnp.concatenate(pieces, axis=0))
            slope = jnp.concatenate(strips, axis=1)
            high = slope.astype(bf16)
            low = (slope - high.astype(f32)).astype(bf16)
            lg_hi[pl.ds(base, row_width), :] = high
            lg_lo[pl.ds(base, row_width), :] = low
            dims = (((1,), (1,)), ((), ()))
            both = lax.dot_general(
                col_right[dim_pad : 3 * dim_pad, :], high, dims, preferred_element_type=f32
            )
            rest = lax.dot_general(col_right[0:dim_pad, :], low, dims, preferred_element_type=f32)
            row_sum[q] = row_sum[q] + (both[0:dim_pad] + (both[dim_pad:] + rest))

        @pl.when(step == 2 * chips - 1)
        def _():
            @pl.loop(1, n_col)
            def _(k):
                row_copy(k).start()

        both = jnp.dot(row_left[0 : 2 * dim_pad, :], lg_hi[...], preferred_element_type=f32)
        rest = jnp.dot(row_left[0:dim_pad, :], lg_lo[...], preferred_element_type=f32)
        col_out[step] = both[0:dim_pad] + (both[dim_pad:] + rest)

        @pl.when(second == 0)
        def _():
            pair_copy(t).start()

        @pl.when(second == 1)
        def _():
            pair_copy(t).wait_recv()
            col_out[step] = col_out[step] + pair_in[t]

            @pl.when(t < chips - 1)
            def _():
                chip_copy(t).start()

    total = col_out[2 * chips - 1]
    for t in range(chips - 1):
        chip_copy(t).wait_recv()
        total = total + chip_in[t]
    col_share[...] = total[0:dim]
    row_total = row_sum[c]
    for k in range(1, n_col):
        row_copy(k).wait_recv()
        row_total = row_total + row_in[k]
    row_share[...] = row_total[0:dim]

    @pl.loop(0, chips)
    def _(t):
        pair_copy(t).wait_send()

    @pl.loop(0, chips - 1)
    def _(t):
        chip_copy(t).wait_send()

    @pl.loop(1, n_col)
    def _(k):
        row_copy(k).wait_send()


def gradients(n_row, n_col, half_scale, table, rows, cols, gain, offset, row_log, col_log):
    f32 = jnp.float32
    bf16 = jnp.bfloat16
    dim, row_width = rows.shape[1:]
    col_width = cols.shape[2]
    dim_pad = round_up(dim, 16)
    depth = round_up(3 * dim_pad, 128)
    tile_rows = n_col * row_width
    chips = n_row // 2
    smem = pl.BlockSpec(memory_space=pltpu.SMEM)
    vmem = pl.BlockSpec(memory_space=pltpu.VMEM)
    dma = pltpu.SemaphoreType.DMA
    return pl.pallas_call(
        functools.partial(gradient_kernel, n_row, n_col, dim, dim_pad, depth, half_scale),
        out_shape=(
            jax.ShapeDtypeStruct((dim, row_width), f32),
            jax.ShapeDtypeStruct((dim, col_width), f32),
        ),
        in_specs=[smem] + [vmem] * 6,
        out_specs=(vmem,) * 2,
        scratch_shapes=[
            pltpu.VMEM((dim_pad, row_width), f32),
            pltpu.VMEM((dim_pad, col_width), f32),
            pltpu.VMEM((depth, tile_rows), bf16),
            pltpu.VMEM((tile_rows, depth), bf16),
            pltpu.VMEM((depth, col_width), bf16),
            pltpu.VMEM((tile_rows, col_width), bf16),
            pltpu.VMEM((tile_rows, col_width), bf16),
            pltpu.VMEM((n_col, dim_pad, row_width), f32),
            pltpu.VMEM((2 * chips, dim_pad, col_width), f32),
            pltpu.VMEM((chips, dim_pad, col_width), f32),
            pltpu.VMEM((max(chips - 1, 1), dim_pad, col_width), f32),
            pltpu.VMEM((n_col, dim_pad, row_width), f32),
            dma((chips,)), dma((chips,)), dma((chips,)), dma((chips,)), dma((n_col,)), dma((n_col,)),
        ],
        compiler_params=pltpu.CompilerParams(
            collective_id=2, has_side_effects=True, vmem_limit_bytes=VMEM_LIMIT
        ),
        name="gradients",
    )(table, rows, cols, gain, offset, row_log, col_log)


def per_device(blocks, plan, live, row_emb, col_emb, row_acc, col_acc):
    n_row = lax.axis_size("row")
    n_col = lax.axis_size("col")
    sub_rows, sub_cols = blocks.shape[5:]
    tile_rows = row_emb.shape[1] * n_col
    tile_cols = col_emb.shape[1] * n_row
    scale = 4.0 * float(tile_rows * n_row * tile_cols * n_col) ** (-0.25)
    arrived, rows, cols = exchange(n_row, n_col, blocks[0, 0], row_emb, col_emb)
    places = plan[0, 0]
    slot_ids = lax.broadcasted_iota(jnp.int32, places.shape, 2)
    alive = (slot_ids < live[0, 0][:, :, None]).astype(jnp.int32)
    gain, offset, table, row_part, col_part = merge(
        scale, places.reshape(-1), alive.reshape(-1), arrived.reshape(-1, sub_rows, sub_cols),
        tile_rows // sub_rows, tile_cols // sub_cols,
    )
    row_log, col_log = masses(n_row, n_col, row_part, col_part)
    row_wide = jnp.broadcast_to(row_log.reshape(tile_rows, 1), (tile_rows, sub_cols))
    row_share, col_share = gradients(
        n_row, n_col, 0.5 * scale, table, rows, cols, gain, offset, row_wide, col_log
    )
    new_row_acc = row_acc + row_share * row_share
    new_col_acc = col_acc + col_share * col_share
    new_row_emb = row_emb - LEARNING_RATE * row_share / jnp.sqrt(new_row_acc)
    new_col_emb = col_emb - LEARNING_RATE * col_share / jnp.sqrt(new_col_acc)
    return (new_row_emb, new_col_emb, new_row_acc, new_col_acc)


def solution(mesh):
    return jax.shard_map(
        per_device,
        mesh=mesh,
        in_specs=(
            P("row", "col", None, None, None, None, None),
            P("row", "col", None, None, None),
            P("row", "col", None, None),
            P(None, ("row", "col")),
            P(None, ("col", "row")),
            P(None, ("row", "col")),
            P(None, ("col", "row")),
        ),
        out_specs=(
            P(None, ("row", "col")),
            P(None, ("col", "row")),
            P(None, ("row", "col")),
            P(None, ("col", "row")),
        ),
        check_vma=False,
    )
```

```python
import functools

import jax
import jax.numpy as jnp
from jax import lax
from jax.experimental import pallas as pl
from jax.experimental.pallas import tpu as pltpu
from jax.sharding import PartitionSpec as P

LEARNING_RATE = 0.2
MESH = pl.DeviceIdType.MESH
VMEM_LIMIT = 56 * 1024 * 1024


def round_up(value, step):
    return -(-value // step) * step


def remote(src, dst, send_sem, recv_sem, device):
    return pltpu.make_async_remote_copy(
        src_ref=src, dst_ref=dst, send_sem=send_sem, recv_sem=recv_sem,
        device_id=device, device_id_type=MESH,
    )


def exchange_kernel(
    n_row, n_col, blocks, row_emb, col_emb, arrived, rows, cols,
    a_send, a_recv, r_send, r_recv, d_send, d_recv, c_send, c_recv, f_send, f_recv, local_sem,
):
    r = lax.axis_index("row")
    c = lax.axis_index("col")
    core = lax.rem(r, 2)
    sibling = r + 1 - 2 * core
    chips = n_row // 2
    total = n_row * n_col

    def peer(k):
        return lax.rem(r + k % n_row, n_row), lax.rem(c + k // n_row, n_col)

    def chip_peer(t):
        return lax.rem(r + 2 * t, n_row)

    barrier = pltpu.get_barrier_semaphore()

    @pl.loop(1, total)
    def _(k):
        pl.semaphore_signal(barrier, inc=1, device_id=peer(k), device_id_type=MESH)

    pl.semaphore_wait(barrier, total - 1)

    local = [
        pltpu.make_async_copy(blocks.at[c, r], arrived.at[c, r], local_sem.at[0]),
        pltpu.make_async_copy(row_emb, rows.at[c], local_sem.at[1]),
        pltpu.make_async_copy(col_emb, cols.at[r], local_sem.at[2]),
    ]

    after = (r, lax.rem(c + 1, n_col))
    before = (r, lax.rem(c + n_col - 1, n_col))

    def up(k):
        shard = lax.rem(c + n_col - k + 1, n_col)
        source = row_emb if k == 1 else rows.at[shard]
        return remote(source, rows.at[shard], r_send.at[k], r_recv.at[k], after)

    def down(k):
        shard = lax.rem(c + k - 1, n_col)
        source = row_emb if k == 1 else rows.at[shard]
        return remote(source, rows.at[shard], d_send.at[k], d_recv.at[k], before)

    def sends_up(k):
        return jnp.logical_and(c + 1 < n_col, c >= k - 1)

    def sends_down(k):
        return jnp.logical_and(c >= 1, c + k - 1 < n_col)

    def col_copy(t):
        return remote(col_emb, cols.at[r], c_send.at[t], c_recv.at[t], (chip_peer(t), c))

    def pair_copy():
        return remote(col_emb, cols.at[r], f_send.at[0], f_recv.at[0], (sibling, c))

    def forward(t):
        origin = lax.rem(r + n_row - 2 * t, n_row)
        return remote(cols.at[origin], cols.at[origin], f_send.at[t], f_recv.at[t], (sibling, c))

    def block_copy(k):
        pr, pc = peer(k)
        return remote(blocks.at[pc, pr], arrived.at[c, r], a_send.at[k], a_recv.at[k], (pr, pc))

    @pl.when(sends_up(1))
    def _():
        up(1).start()

    @pl.when(sends_down(1))
    def _():
        down(1).start()

    @pl.loop(1, chips)
    def _(t):
        col_copy(t).start()

    pair_copy().start()

    @pl.loop(1, total)
    def _(k):
        block_copy(total - k).start()

    for copy in local:
        copy.start()

    for k in range(1, n_col):

        @pl.when(c >= k)
        def _():
            up(k).wait_recv()

        @pl.when(c + k < n_col)
        def _():
            down(k).wait_recv()

        if k + 1 < n_col:

            @pl.when(sends_up(k + 1))
            def _():
                up(k + 1).start()

            @pl.when(sends_down(k + 1))
            def _():
                down(k + 1).start()

    @pl.loop(1, chips)
    def _(t):
        col_copy(t).wait_recv()
        forward(t).start()

    for copy in local:
        copy.wait()
    pair_copy().wait()

    @pl.loop(1, chips)
    def _(t):
        col_copy(t).wait_send()
        forward(t).wait()

    for k in range(1, n_col):

        @pl.when(sends_up(k))
        def _():
            up(k).wait_send()

        @pl.when(sends_down(k))
        def _():
            down(k).wait_send()

    @pl.loop(1, total)
    def _(k):
        block_copy(k).wait()


def exchange(n_row, n_col, blocks, row_emb, col_emb):
    f32 = jnp.float32
    any_spec = pl.BlockSpec(memory_space=pl.ANY)
    dma = pltpu.SemaphoreType.DMA
    total = n_row * n_col
    return pl.pallas_call(
        functools.partial(exchange_kernel, n_row, n_col),
        out_shape=(
            jax.ShapeDtypeStruct(blocks.shape, f32),
            jax.ShapeDtypeStruct((n_col,) + row_emb.shape, f32),
            jax.ShapeDtypeStruct((n_row,) + col_emb.shape, f32),
        ),
        in_specs=[any_spec] * 3,
        out_specs=(any_spec,) * 3,
        scratch_shapes=[
            dma((total,)), dma((total,)), dma((n_col,)), dma((n_col,)), dma((n_col,)), dma((n_col,)),
            dma((n_row // 2,)), dma((n_row // 2,)), dma((n_row // 2,)), dma((n_row // 2,)), dma((3,)),
        ],
        compiler_params=pltpu.CompilerParams(collective_id=0, has_side_effects=True),
        name="exchange",
    )(blocks, row_emb, col_emb)


def merge_kernel(scale, plan, live, blocks, gain, offset, table, row_part, col_part, row_sum, seen):
    slots, sub_rows, sub_cols = blocks.shape
    places = table.shape[0]
    grid_columns = col_part.shape[0]

    @pl.loop(0, places)
    def _(b):
        table[b] = slots

    row_sum[...] = jnp.zeros_like(row_sum)
    col_part[...] = jnp.zeros_like(col_part)
    gain[slots] = jnp.zeros((sub_rows, sub_cols), jnp.float32)
    offset[slots] = jnp.zeros((sub_rows, sub_cols), jnp.float32)

    @pl.loop(0, slots)
    def _(k):
        @pl.when(live[k] > 0)
        def _():
            place = plan[k]
            i = place // grid_columns
            j = place - i * grid_columns
            block = blocks[k]
            row_sum[i] = row_sum[i] + block
            col_part[pl.ds(j, 1), :] += jnp.sum(block, axis=0, keepdims=True)
            first = table[place]
            fresh = first == slots
            target = jnp.where(fresh, k, first)
            table[place] = target

            @pl.when(fresh)
            def _():
                seen[k] = block

            @pl.when(jnp.logical_not(fresh))
            def _():
                seen[target] = seen[target] + block
                seen[k] = block

        @pl.when(live[k] <= 0)
        def _():
            seen[k] = jnp.ones((sub_rows, sub_cols), jnp.float32)

    @pl.loop(0, slots)
    def _(k):
        counts = seen[k]
        confidence = scale * (0.1 + 0.25 * jnp.sqrt(counts))
        gain[k] = confidence
        offset[k] = -confidence * jnp.log(counts)

    row_part[...] = jnp.sum(row_sum[...], axis=2)


def merge(scale, plan, live, blocks, grid_rows, grid_columns):
    slots, sub_rows, sub_cols = blocks.shape
    f32 = jnp.float32
    smem = pl.BlockSpec(memory_space=pltpu.SMEM)
    vmem = pl.BlockSpec(memory_space=pltpu.VMEM)
    return pl.pallas_call(
        functools.partial(merge_kernel, scale),
        out_shape=(
            jax.ShapeDtypeStruct((slots + 1, sub_rows, sub_cols), f32),
            jax.ShapeDtypeStruct((slots + 1, sub_rows, sub_cols), f32),
            jax.ShapeDtypeStruct((grid_rows * grid_columns,), jnp.int32),
            jax.ShapeDtypeStruct((grid_rows, sub_rows), f32),
            jax.ShapeDtypeStruct((grid_columns, sub_cols), f32),
        ),
        in_specs=[smem, smem, vmem],
        out_specs=(vmem, vmem, smem, vmem, vmem),
        scratch_shapes=[
            pltpu.VMEM((grid_rows, sub_rows, sub_cols), f32),
            pltpu.VMEM((slots, sub_rows, sub_cols), f32),
        ],
        compiler_params=pltpu.CompilerParams(vmem_limit_bytes=VMEM_LIMIT),
        name="merge",
    )(plan, live, blocks)


def mass_kernel(
    n_row, n_col, row_part, col_part, row_log, col_log, row_in, col_in, tot_out, tot_in,
    r_send, r_recv, c_send, c_recv, t_send, t_recv,
):
    r = lax.axis_index("row")
    c = lax.axis_index("col")

    def row_peer(k):
        return (lax.rem(r + k, n_row), c)

    def col_peer(k):
        return (r, lax.rem(c + k, n_col))

    barrier = pltpu.get_barrier_semaphore()

    @pl.loop(1, n_row)
    def _(k):
        pl.semaphore_signal(barrier, inc=1, device_id=row_peer(k), device_id_type=MESH)

    @pl.loop(1, n_col)
    def _(k):
        pl.semaphore_signal(barrier, inc=1, device_id=col_peer(k), device_id_type=MESH)

    pl.semaphore_wait(barrier, n_row + n_col - 2)

    def col_copy(k):
        return remote(col_part, col_in.at[k], c_send.at[k], c_recv.at[k], row_peer(k))

    def row_copy(k):
        return remote(row_part, row_in.at[k], r_send.at[k], r_recv.at[k], col_peer(k))

    def tot_copy(k):
        return remote(tot_out, tot_in.at[k], t_send.at[k], t_recv.at[k], col_peer(k))

    @pl.loop(1, n_row)
    def _(k):
        col_copy(k).start()

    @pl.loop(1, n_col)
    def _(k):
        row_copy(k).start()

    @pl.loop(1, n_row)
    def _(k):
        col_copy(k).wait()

    col_mass = col_part[...]
    for k in range(1, n_row):
        col_mass = col_mass + col_in[k]
    part = jnp.sum(jnp.sum(col_mass, axis=0, keepdims=True), axis=1, keepdims=True)
    tot_out[...] = jnp.broadcast_to(part, tot_out.shape)

    @pl.loop(1, n_col)
    def _(k):
        tot_copy(k).start()

    @pl.loop(1, n_col)
    def _(k):
        row_copy(k).wait()

    row_mass = row_part[...]
    for k in range(1, n_col):
        row_mass = row_mass + row_in[k]
    row_log[...] = jnp.log(row_mass)

    @pl.loop(1, n_col)
    def _(k):
        tot_copy(k).wait()

    grand = tot_out[...]
    for k in range(1, n_col):
        grand = grand + tot_in[k]
    col_log[...] = jnp.log(col_mass) - jnp.log(grand[0:1, :])


def masses(n_row, n_col, row_part, col_part):
    f32 = jnp.float32
    vmem = pl.BlockSpec(memory_space=pltpu.VMEM)
    dma = pltpu.SemaphoreType.DMA
    return pl.pallas_call(
        functools.partial(mass_kernel, n_row, n_col),
        out_shape=(
            jax.ShapeDtypeStruct(row_part.shape, f32),
            jax.ShapeDtypeStruct(col_part.shape, f32),
        ),
        in_specs=[vmem] * 2,
        out_specs=(vmem,) * 2,
        scratch_shapes=[
            pltpu.VMEM((n_col,) + row_part.shape, f32),
            pltpu.VMEM((n_row,) + col_part.shape, f32),
            pltpu.VMEM((8, col_part.shape[1]), f32),
            pltpu.VMEM((n_col, 8, col_part.shape[1]), f32),
            dma((n_col,)), dma((n_col,)), dma((n_row,)), dma((n_row,)), dma((n_col,)), dma((n_col,)),
        ],
        compiler_params=pltpu.CompilerParams(collective_id=1, has_side_effects=True),
        name="masses",
    )(row_part, col_part)


def gradient_kernel(
    n_row, n_col, dim, dim_pad, depth, half_scale,
    table, rows, cols, gain, offset, row_log, col_log, row_share, col_share,
    pad_row, pad_col, row_left, row_turned, right_0, right_1, score_0, score_1, lg_hi, lg_lo,
    row_sum, col_out, pair_in, chip_in, row_in,
    p_send, p_recv, h_send, h_recv, r_send, r_recv,
):
    f32 = jnp.float32
    bf16 = jnp.bfloat16
    r = lax.axis_index("row")
    c = lax.axis_index("col")
    core = lax.rem(r, 2)
    chip = r // 2
    chips = n_row // 2
    sibling = r + 1 - 2 * core
    row_width = rows.shape[2]
    col_width = cols.shape[2]
    sub_rows, sub_cols = gain.shape[1:]
    per_chunk = col_width // sub_cols
    grid_columns = col_log.shape[0]
    halves, _, _, piece = row_sum.shape
    lines = piece // sub_rows
    shard_lines = row_width // sub_rows

    barrier = pltpu.get_barrier_semaphore()
    pl.semaphore_signal(barrier, inc=1, device_id=(sibling, c), device_id_type=MESH)

    @pl.loop(1, chips)
    def _(t):
        pl.semaphore_signal(barrier, inc=1, device_id=(lax.rem(r + 2 * t, n_row), c), device_id_type=MESH)

    @pl.loop(1, n_col)
    def _(k):
        pl.semaphore_signal(barrier, inc=1, device_id=(r, lax.rem(c + k, n_col)), device_id_type=MESH)

    pl.semaphore_wait(barrier, chips + n_col - 1)

    def pair_copy(t):
        return remote(col_out.at[2 * t], pair_in.at[t], p_send.at[t], p_recv.at[t], (sibling, c))

    def chip_copy(t):
        return remote(
            col_out.at[2 * t + 1], chip_in.at[t], h_send.at[t], h_recv.at[t],
            (lax.rem(r + 2 * (t + 1), n_row), c),
        )

    def row_copy(h, k):
        target = lax.rem(c + k, n_col)
        sem = h * n_col + k
        return remote(
            row_sum.at[h, target], row_in.at[h, k], r_send.at[sem], r_recv.at[sem], (r, target)
        )

    def split(value):
        high = value.astype(bf16)
        return high, (value - high.astype(f32)).astype(bf16)

    def chunk_at(u, second):
        t = lax.rem(u, chips)
        return 2 * lax.rem(chip + 1 + t, chips) + (core if second else 1 - core)

    def prepare(u, second, right, score):
        pad_col[0:dim, :] = cols[chunk_at(u, second)]
        high, low = split(pad_col[...])
        right[0:dim_pad, :] = high
        right[dim_pad : 2 * dim_pad, :] = high
        right[2 * dim_pad : 3 * dim_pad, :] = low
        score[...] = jnp.dot(row_turned[u // chips], right[...], preferred_element_type=f32)

    def work(u, second, right, score):
        h = u // chips
        chunk = chunk_at(u, second)
        step = 2 * lax.rem(u, chips) + second
        for j in range(per_chunk):
            column = chunk * per_chunk + j
            col_base = col_log[pl.ds(column, 1), :]
            across = slice(j * sub_cols, (j + 1) * sub_cols)
            for q in range(n_col):
                values = []
                for i in range(lines):
                    line = q * shard_lines + h * lines + i
                    slot = table[line * grid_columns + column]
                    a = gain[slot]
                    b = offset[slot]
                    row_base = row_log[pl.ds(pl.multiple_of(line * sub_rows, sub_rows), sub_rows), :]
                    at = q * piece + i * sub_rows
                    x = score[at : at + sub_rows, across] + (row_base + col_base)
                    values.append(
                        jnp.where(a > 0, a * x + b, half_scale + half_scale * jnp.tanh(0.5 * x))
                    )
                high, low = split(jnp.concatenate(values, axis=0))
                lg_hi[q * piece : (q + 1) * piece, across] = high
                lg_lo[q * piece : (q + 1) * piece, across] = low
        dims = (((1,), (1,)), ((), ()))
        both = lax.dot_general(
            right[dim_pad : 3 * dim_pad, :], lg_hi[...], dims, preferred_element_type=f32
        )
        rest = lax.dot_general(right[0:dim_pad, :], lg_lo[...], dims, preferred_element_type=f32)
        row_new = both[0:dim_pad] + (both[dim_pad:] + rest)
        for q in range(n_col):
            row_sum[h, q] = row_sum[h, q] + row_new[:, q * piece : (q + 1) * piece]
        left = row_left.at[h]
        both = jnp.dot(left[0 : 2 * dim_pad, :], lg_hi[...], preferred_element_type=f32)
        rest = jnp.dot(left[0:dim_pad, :], lg_lo[...], preferred_element_type=f32)
        col_out[step] = col_out[step] + (both[0:dim_pad] + (both[dim_pad:] + rest))

    pad_row[...] = jnp.zeros_like(pad_row)
    pad_col[...] = jnp.zeros_like(pad_col)
    row_left[...] = jnp.zeros_like(row_left)
    right_0[...] = jnp.zeros_like(right_0)
    right_1[...] = jnp.zeros_like(right_1)
    row_sum[...] = jnp.zeros_like(row_sum)

    @pl.loop(0, 2 * chips)
    def _(step):
        col_out[step] = jnp.zeros(col_out.shape[1:], f32)

    for q in range(n_col):
        pad_row[0:dim, :] = rows[q]
        high, low = split(pad_row[...])
        for h in range(halves):
            span = slice(q * piece, (q + 1) * piece)
            part = slice(h * piece, (h + 1) * piece)
            row_left[h, 0:dim_pad, span] = high[:, part]
            row_left[h, dim_pad : 2 * dim_pad, span] = low[:, part]
            row_left[h, 2 * dim_pad : 3 * dim_pad, span] = high[:, part]
            row_turned[h, span, :] = row_left[h, :, span].T

    prepare(0, 0, right_0, score_0)

    @pl.loop(0, halves * chips)
    def _(u):
        t = lax.rem(u, chips)
        last = u >= (halves - 1) * chips
        prepare(u, 1, right_1, score_1)
        work(u, 0, right_0, score_0)

        @pl.when(last)
        def _():
            pair_copy(t).start()

        prepare(jnp.minimum(u + 1, halves * chips - 1), 0, right_0, score_0)
        work(u, 1, right_1, score_1)

        @pl.when(t == chips - 1)
        def _():
            @pl.loop(1, n_col)
            def _(k):
                row_copy(u // chips, k).start()

        @pl.when(last)
        def _():
            pair_copy(t).wait_recv()
            col_out[2 * t + 1] = col_out[2 * t + 1] + pair_in[t]

            @pl.when(t < chips - 1)
            def _():
                chip_copy(t).start()

    total = col_out[2 * chips - 1]
    for t in range(chips - 1):
        chip_copy(t).wait_recv()
        total = total + chip_in[t]
    col_share[...] = total[0:dim]
    for h in range(halves):
        row_total = row_sum[h, c]
        for k in range(1, n_col):
            row_copy(h, k).wait_recv()
            row_total = row_total + row_in[h, k]
        row_share[:, h * piece : (h + 1) * piece] = row_total[0:dim]

    @pl.loop(0, chips)
    def _(t):
        pair_copy(t).wait_send()

    @pl.loop(0, chips - 1)
    def _(t):
        chip_copy(t).wait_send()

    for h in range(halves):

        @pl.loop(1, n_col)
        def _(k):
            row_copy(h, k).wait_send()


def gradients(n_row, n_col, half_scale, table, rows, cols, gain, offset, row_log, col_log):
    f32 = jnp.float32
    bf16 = jnp.bfloat16
    dim, row_width = rows.shape[1:]
    col_width = cols.shape[2]
    dim_pad = round_up(dim, 16)
    depth = round_up(3 * dim_pad, 128)
    halves = 2 if row_width % 256 == 0 else 1
    piece = row_width // halves
    half_rows = n_col * piece
    chips = n_row // 2
    smem = pl.BlockSpec(memory_space=pltpu.SMEM)
    vmem = pl.BlockSpec(memory_space=pltpu.VMEM)
    dma = pltpu.SemaphoreType.DMA
    return pl.pallas_call(
        functools.partial(gradient_kernel, n_row, n_col, dim, dim_pad, depth, half_scale),
        out_shape=(
            jax.ShapeDtypeStruct((dim, row_width), f32),
            jax.ShapeDtypeStruct((dim, col_width), f32),
        ),
        in_specs=[smem] + [vmem] * 6,
        out_specs=(vmem,) * 2,
        scratch_shapes=[
            pltpu.VMEM((dim_pad, row_width), f32),
            pltpu.VMEM((dim_pad, col_width), f32),
            pltpu.VMEM((halves, depth, half_rows), bf16),
            pltpu.VMEM((halves, half_rows, depth), bf16),
            pltpu.VMEM((depth, col_width), bf16),
            pltpu.VMEM((depth, col_width), bf16),
            pltpu.VMEM((half_rows, col_width), f32),
            pltpu.VMEM((half_rows, col_width), f32),
            pltpu.VMEM((half_rows, col_width), bf16),
            pltpu.VMEM((half_rows, col_width), bf16),
            pltpu.VMEM((halves, n_col, dim_pad, piece), f32),
            pltpu.VMEM((2 * chips, dim_pad, col_width), f32),
            pltpu.VMEM((chips, dim_pad, col_width), f32),
            pltpu.VMEM((max(chips - 1, 1), dim_pad, col_width), f32),
            pltpu.VMEM((halves, n_col, dim_pad, piece), f32),
            dma((chips,)), dma((chips,)), dma((chips,)), dma((chips,)),
            dma((halves * n_col,)), dma((halves * n_col,)),
        ],
        compiler_params=pltpu.CompilerParams(
            collective_id=2, has_side_effects=True, vmem_limit_bytes=VMEM_LIMIT
        ),
        name="gradients",
    )(table, rows, cols, gain, offset, row_log, col_log)


def per_device(blocks, plan, live, row_emb, col_emb, row_acc, col_acc):
    n_row = lax.axis_size("row")
    n_col = lax.axis_size("col")
    sub_rows, sub_cols = blocks.shape[5:]
    tile_rows = row_emb.shape[1] * n_col
    tile_cols = col_emb.shape[1] * n_row
    scale = 4.0 * float(tile_rows * n_row * tile_cols * n_col) ** (-0.25)
    arrived, rows, cols = exchange(n_row, n_col, blocks[0, 0], row_emb, col_emb)
    places = plan[0, 0]
    slot_ids = lax.broadcasted_iota(jnp.int32, places.shape, 2)
    alive = (slot_ids < live[0, 0][:, :, None]).astype(jnp.int32)
    gain, offset, table, row_part, col_part = merge(
        scale, places.reshape(-1), alive.reshape(-1), arrived.reshape(-1, sub_rows, sub_cols),
        tile_rows // sub_rows, tile_cols // sub_cols,
    )
    row_log, col_log = masses(n_row, n_col, row_part, col_part)
    row_wide = jnp.broadcast_to(row_log.reshape(tile_rows, 1), (tile_rows, sub_cols))
    row_share, col_share = gradients(
        n_row, n_col, 0.5 * scale, table, rows, cols, gain, offset, row_wide, col_log
    )
    new_row_acc = row_acc + row_share * row_share
    new_col_acc = col_acc + col_share * col_share
    new_row_emb = row_emb - LEARNING_RATE * row_share / jnp.sqrt(new_row_acc)
    new_col_emb = col_emb - LEARNING_RATE * col_share / jnp.sqrt(new_col_acc)
    return (new_row_emb, new_col_emb, new_row_acc, new_col_acc)


def solution(mesh):
    return jax.shard_map(
        per_device,
        mesh=mesh,
        in_specs=(
            P("row", "col", None, None, None, None, None),
            P("row", "col", None, None, None),
            P("row", "col", None, None),
            P(None, ("row", "col")),
            P(None, ("col", "row")),
            P(None, ("row", "col")),
            P(None, ("col", "row")),
        ),
        out_specs=(
            P(None, ("row", "col")),
            P(None, ("col", "row")),
            P(None, ("row", "col")),
            P(None, ("col", "row")),
        ),
        check_vma=False,
    )
```

```python
import functools

import jax
import jax.numpy as jnp
from jax import lax
from jax.experimental import pallas as pl
from jax.experimental.pallas import tpu as pltpu
from jax.sharding import PartitionSpec as P

LEARNING_RATE = 0.2
MESH = pl.DeviceIdType.MESH
VMEM_LIMIT = 56 * 1024 * 1024


def round_up(value, step):
    return -(-value // step) * step


def remote(src, dst, send_sem, recv_sem, device):
    return pltpu.make_async_remote_copy(
        src_ref=src, dst_ref=dst, send_sem=send_sem, recv_sem=recv_sem,
        device_id=device, device_id_type=MESH,
    )


def exchange_kernel(
    n_row, n_col, blocks, row_emb, col_emb, arrived, rows, cols,
    a_send, a_recv, r_send, r_recv, d_send, d_recv, c_send, c_recv, f_send, f_recv, local_sem,
):
    r = lax.axis_index("row")
    c = lax.axis_index("col")
    core = lax.rem(r, 2)
    sibling = r + 1 - 2 * core
    chips = n_row // 2
    total = n_row * n_col

    def peer(k):
        return lax.rem(r + k % n_row, n_row), lax.rem(c + k // n_row, n_col)

    def chip_peer(t):
        return lax.rem(r + 2 * t, n_row)

    barrier = pltpu.get_barrier_semaphore()

    @pl.loop(1, total)
    def _(k):
        pl.semaphore_signal(barrier, inc=1, device_id=peer(k), device_id_type=MESH)

    pl.semaphore_wait(barrier, total - 1)

    local = [
        pltpu.make_async_copy(blocks.at[c, r], arrived.at[c, r], local_sem.at[0]),
        pltpu.make_async_copy(row_emb, rows.at[c], local_sem.at[1]),
        pltpu.make_async_copy(col_emb, cols.at[r], local_sem.at[2]),
    ]

    after = (r, lax.rem(c + 1, n_col))
    before = (r, lax.rem(c + n_col - 1, n_col))

    def up(k):
        shard = lax.rem(c + n_col - k + 1, n_col)
        source = row_emb if k == 1 else rows.at[shard]
        return remote(source, rows.at[shard], r_send.at[k], r_recv.at[k], after)

    def down(k):
        shard = lax.rem(c + k - 1, n_col)
        source = row_emb if k == 1 else rows.at[shard]
        return remote(source, rows.at[shard], d_send.at[k], d_recv.at[k], before)

    def sends_up(k):
        return jnp.logical_and(c + 1 < n_col, c >= k - 1)

    def sends_down(k):
        return jnp.logical_and(c >= 1, c + k - 1 < n_col)

    def col_copy(t):
        return remote(col_emb, cols.at[r], c_send.at[t], c_recv.at[t], (chip_peer(t), c))

    def pair_copy():
        return remote(col_emb, cols.at[r], f_send.at[0], f_recv.at[0], (sibling, c))

    def forward(t):
        origin = lax.rem(r + n_row - 2 * t, n_row)
        return remote(cols.at[origin], cols.at[origin], f_send.at[t], f_recv.at[t], (sibling, c))

    def block_copy(k):
        pr, pc = peer(k)
        return remote(blocks.at[pc, pr], arrived.at[c, r], a_send.at[k], a_recv.at[k], (pr, pc))

    @pl.when(sends_up(1))
    def _():
        up(1).start()

    @pl.when(sends_down(1))
    def _():
        down(1).start()

    @pl.loop(1, chips)
    def _(t):
        col_copy(t).start()

    pair_copy().start()

    @pl.loop(1, total)
    def _(k):
        block_copy(total - k).start()

    for copy in local:
        copy.start()

    for k in range(1, n_col):

        @pl.when(c >= k)
        def _():
            up(k).wait_recv()

        @pl.when(c + k < n_col)
        def _():
            down(k).wait_recv()

        if k + 1 < n_col:

            @pl.when(sends_up(k + 1))
            def _():
                up(k + 1).start()

            @pl.when(sends_down(k + 1))
            def _():
                down(k + 1).start()

    @pl.loop(1, chips)
    def _(t):
        col_copy(t).wait_recv()
        forward(t).start()

    for copy in local:
        copy.wait()
    pair_copy().wait()

    @pl.loop(1, chips)
    def _(t):
        col_copy(t).wait_send()
        forward(t).wait()

    for k in range(1, n_col):

        @pl.when(sends_up(k))
        def _():
            up(k).wait_send()

        @pl.when(sends_down(k))
        def _():
            down(k).wait_send()

    @pl.loop(1, total)
    def _(k):
        block_copy(k).wait()


def exchange(n_row, n_col, blocks, row_emb, col_emb):
    f32 = jnp.float32
    any_spec = pl.BlockSpec(memory_space=pl.ANY)
    dma = pltpu.SemaphoreType.DMA
    total = n_row * n_col
    return pl.pallas_call(
        functools.partial(exchange_kernel, n_row, n_col),
        out_shape=(
            jax.ShapeDtypeStruct(blocks.shape, f32),
            jax.ShapeDtypeStruct((n_col,) + row_emb.shape, f32),
            jax.ShapeDtypeStruct((n_row,) + col_emb.shape, f32),
        ),
        in_specs=[any_spec] * 3,
        out_specs=(any_spec,) * 3,
        scratch_shapes=[
            dma((total,)), dma((total,)), dma((n_col,)), dma((n_col,)), dma((n_col,)), dma((n_col,)),
            dma((n_row // 2,)), dma((n_row // 2,)), dma((n_row // 2,)), dma((n_row // 2,)), dma((3,)),
        ],
        compiler_params=pltpu.CompilerParams(collective_id=0, has_side_effects=True),
        name="exchange",
    )(blocks, row_emb, col_emb)


def merge_kernel(
    scale, plan, live, blocks, gain, offset, table, row_part, col_part, row_sum, col_sum, seen
):
    slots, sub_rows, sub_cols = blocks.shape
    places = table.shape[0]
    grid_columns = col_part.shape[0]

    @pl.loop(0, places, unroll=8)
    def _(b):
        table[b] = slots

    row_sum[...] = jnp.zeros_like(row_sum)
    col_sum[...] = jnp.zeros_like(col_sum)
    gain[slots] = jnp.zeros((sub_rows, sub_cols), jnp.float32)
    offset[slots] = jnp.zeros((sub_rows, sub_cols), jnp.float32)

    @pl.loop(0, slots)
    def _(k):
        @pl.when(live[k] > 0)
        def _():
            place = plan[k]
            i = place // grid_columns
            j = place - i * grid_columns
            block = blocks[k]
            first = table[place]
            fresh = first == slots
            target = jnp.where(fresh, k, first)
            table[place] = target
            row_sum[i] = row_sum[i] + block
            col_sum[j] = col_sum[j] + jnp.sum(block.reshape(sub_rows // 8, 8, sub_cols), axis=0)
            seen[target] = jnp.where(fresh, block, seen[target] + block)

    @pl.loop(0, slots, unroll=4)
    def _(k):
        counts = seen[k]
        confidence = scale * (0.1 + 0.25 * jnp.sqrt(counts))
        gain[k] = confidence
        offset[k] = -confidence * jnp.log(counts)

    row_part[...] = jnp.sum(row_sum[...], axis=2)
    col_part[...] = jnp.sum(col_sum[...], axis=1)


def merge(scale, plan, live, blocks, grid_rows, grid_columns):
    slots, sub_rows, sub_cols = blocks.shape
    f32 = jnp.float32
    smem = pl.BlockSpec(memory_space=pltpu.SMEM)
    vmem = pl.BlockSpec(memory_space=pltpu.VMEM)
    return pl.pallas_call(
        functools.partial(merge_kernel, scale),
        out_shape=(
            jax.ShapeDtypeStruct((slots + 1, sub_rows, sub_cols), f32),
            jax.ShapeDtypeStruct((slots + 1, sub_rows, sub_cols), f32),
            jax.ShapeDtypeStruct((grid_rows * grid_columns,), jnp.int32),
            jax.ShapeDtypeStruct((grid_rows, sub_rows), f32),
            jax.ShapeDtypeStruct((grid_columns, sub_cols), f32),
        ),
        in_specs=[smem, smem, vmem],
        out_specs=(vmem, vmem, smem, vmem, vmem),
        scratch_shapes=[
            pltpu.VMEM((grid_rows, sub_rows, sub_cols), f32),
            pltpu.VMEM((grid_columns, 8, sub_cols), f32),
            pltpu.VMEM((slots, sub_rows, sub_cols), f32),
        ],
        compiler_params=pltpu.CompilerParams(vmem_limit_bytes=VMEM_LIMIT),
        name="merge",
    )(plan, live, blocks)


def gradient_kernel(
    n_row, n_col, dim, dim_pad, depth, half_scale,
    table, rows, cols, gain, offset, row_part, col_part, row_share, col_share,
    row_log, col_log, mass_row, mass_col, mass_out, mass_tot,
    pad_row, pad_col, row_left, row_turned, right_0, right_1, score_0, score_1, lg_hi, lg_lo,
    row_sum, col_out, pair_in, chip_in, row_in,
    p_send, p_recv, h_send, h_recv, r_send, r_recv, mr_send, mr_recv, mc_send, mc_recv, mt_send, mt_recv,
):
    f32 = jnp.float32
    bf16 = jnp.bfloat16
    r = lax.axis_index("row")
    c = lax.axis_index("col")
    core = lax.rem(r, 2)
    chip = r // 2
    chips = n_row // 2
    sibling = r + 1 - 2 * core
    row_width = rows.shape[2]
    col_width = cols.shape[2]
    sub_rows, sub_cols = gain.shape[1:]
    per_chunk = col_width // sub_cols
    grid_columns = col_log.shape[0]
    halves, _, _, piece = row_sum.shape
    lines = piece // sub_rows
    shard_lines = row_width // sub_rows

    barrier = pltpu.get_barrier_semaphore()
    def row_peer(k):
        return (lax.rem(r + k, n_row), c)

    def col_peer(k):
        return (r, lax.rem(c + k, n_col))

    @pl.loop(1, n_row)
    def _(k):
        pl.semaphore_signal(barrier, inc=1, device_id=row_peer(k), device_id_type=MESH)

    @pl.loop(1, n_col)
    def _(k):
        pl.semaphore_signal(barrier, inc=1, device_id=col_peer(k), device_id_type=MESH)

    def col_mass_copy(k):
        return remote(col_part, mass_col.at[k], mc_send.at[k], mc_recv.at[k], row_peer(k))

    def row_mass_copy(k):
        return remote(row_part, mass_row.at[k], mr_send.at[k], mr_recv.at[k], col_peer(k))

    def tot_copy(k):
        return remote(mass_out, mass_tot.at[k], mt_send.at[k], mt_recv.at[k], col_peer(k))

    def pair_copy(t):
        return remote(col_out.at[2 * t], pair_in.at[t], p_send.at[t], p_recv.at[t], (sibling, c))

    def chip_copy(t):
        return remote(
            col_out.at[2 * t + 1], chip_in.at[t], h_send.at[t], h_recv.at[t],
            (lax.rem(r + 2 * (t + 1), n_row), c),
        )

    def row_copy(h, k):
        target = lax.rem(c + k, n_col)
        sem = h * n_col + k
        return remote(
            row_sum.at[h, target], row_in.at[h, k], r_send.at[sem], r_recv.at[sem], (r, target)
        )

    def split(value):
        high = value.astype(bf16)
        return high, (value - high.astype(f32)).astype(bf16)

    def chunk_at(u, second):
        t = lax.rem(u, chips)
        return 2 * lax.rem(chip + 1 + t, chips) + (core if second else 1 - core)

    def prepare(u, second, right, score):
        pad_col[0:dim, :] = cols[chunk_at(u, second)]
        high, low = split(pad_col[...])
        right[0:dim_pad, :] = high
        right[dim_pad : 2 * dim_pad, :] = high
        right[2 * dim_pad : 3 * dim_pad, :] = low
        score[...] = jnp.dot(row_turned[u // chips], right[...], preferred_element_type=f32)

    def work(u, second, right, score):
        h = u // chips
        chunk = chunk_at(u, second)
        step = 2 * lax.rem(u, chips) + second
        for j in range(per_chunk):
            column = chunk * per_chunk + j
            col_base = col_log[pl.ds(column, 1), :]
            across = slice(j * sub_cols, (j + 1) * sub_cols)
            for q in range(n_col):
                values = []
                for i in range(lines):
                    line = q * shard_lines + h * lines + i
                    slot = table[line * grid_columns + column]
                    a = gain[slot]
                    b = offset[slot]
                    row_base = row_log[pl.ds(pl.multiple_of(line * sub_rows, sub_rows), sub_rows), :]
                    at = q * piece + i * sub_rows
                    x = score[at : at + sub_rows, across] + (row_base + col_base)
                    values.append(
                        jnp.where(a > 0, a * x + b, half_scale + half_scale * jnp.tanh(0.5 * x))
                    )
                high, low = split(jnp.concatenate(values, axis=0))
                lg_hi[q * piece : (q + 1) * piece, across] = high
                lg_lo[q * piece : (q + 1) * piece, across] = low
        dims = (((1,), (1,)), ((), ()))
        both = lax.dot_general(
            right[dim_pad : 3 * dim_pad, :], lg_hi[...], dims, preferred_element_type=f32
        )
        rest = lax.dot_general(right[0:dim_pad, :], lg_lo[...], dims, preferred_element_type=f32)
        row_new = both[0:dim_pad] + (both[dim_pad:] + rest)
        for q in range(n_col):
            row_sum[h, q] = row_sum[h, q] + row_new[:, q * piece : (q + 1) * piece]
        left = row_left.at[h]
        both = jnp.dot(left[0 : 2 * dim_pad, :], lg_hi[...], preferred_element_type=f32)
        rest = jnp.dot(left[0:dim_pad, :], lg_lo[...], preferred_element_type=f32)
        col_out[step] = col_out[step] + (both[0:dim_pad] + (both[dim_pad:] + rest))

    pad_row[...] = jnp.zeros_like(pad_row)
    pad_col[...] = jnp.zeros_like(pad_col)
    row_left[...] = jnp.zeros_like(row_left)
    right_0[...] = jnp.zeros_like(right_0)
    right_1[...] = jnp.zeros_like(right_1)
    row_sum[...] = jnp.zeros_like(row_sum)

    pl.semaphore_wait(barrier, n_row + n_col - 2)

    @pl.loop(1, n_row)
    def _(k):
        col_mass_copy(k).start()

    @pl.loop(1, n_col)
    def _(k):
        row_mass_copy(k).start()

    @pl.loop(0, 2 * chips)
    def _(step):
        col_out[step] = jnp.zeros(col_out.shape[1:], f32)

    for q in range(n_col):
        pad_row[0:dim, :] = rows[q]
        high, low = split(pad_row[...])
        for h in range(halves):
            span = slice(q * piece, (q + 1) * piece)
            part = slice(h * piece, (h + 1) * piece)
            row_left[h, 0:dim_pad, span] = high[:, part]
            row_left[h, dim_pad : 2 * dim_pad, span] = low[:, part]
            row_left[h, 2 * dim_pad : 3 * dim_pad, span] = high[:, part]
            row_turned[h, span, :] = row_left[h, :, span].T

    @pl.loop(1, n_row)
    def _(k):
        col_mass_copy(k).wait()

    col_mass = col_part[...]
    for k in range(1, n_row):
        col_mass = col_mass + mass_col[k]
    part = jnp.sum(jnp.sum(col_mass, axis=0, keepdims=True), axis=1, keepdims=True)
    mass_out[...] = jnp.broadcast_to(part, mass_out.shape)

    @pl.loop(1, n_col)
    def _(k):
        tot_copy(k).start()

    prepare(0, 0, right_0, score_0)

    @pl.loop(1, n_col)
    def _(k):
        row_mass_copy(k).wait()

    row_mass = row_part[...]
    for k in range(1, n_col):
        row_mass = row_mass + mass_row[k]
    logs = jnp.log(row_mass)
    square = (sub_rows, sub_rows)
    diagonal = lax.broadcasted_iota(jnp.int32, square, 0) == lax.broadcasted_iota(jnp.int32, square, 1)
    for i in range(logs.shape[0]):
        spread = jnp.where(diagonal, jnp.broadcast_to(logs[i : i + 1, :], square), 0.0)
        column = jnp.sum(spread, axis=1, keepdims=True)
        row_log[i * sub_rows : (i + 1) * sub_rows, :] = jnp.broadcast_to(column, (sub_rows, sub_cols))

    @pl.loop(1, n_col)
    def _(k):
        tot_copy(k).wait()

    grand = mass_out[...]
    for k in range(1, n_col):
        grand = grand + mass_tot[k]
    col_log[...] = jnp.log(col_mass) - jnp.log(grand[0:1, :])

    @pl.loop(0, halves * chips)
    def _(u):
        t = lax.rem(u, chips)
        last = u >= (halves - 1) * chips
        prepare(u, 1, right_1, score_1)
        work(u, 0, right_0, score_0)

        @pl.when(last)
        def _():
            pair_copy(t).start()

        prepare(jnp.minimum(u + 1, halves * chips - 1), 0, right_0, score_0)
        work(u, 1, right_1, score_1)

        @pl.when(t == chips - 1)
        def _():
            @pl.loop(1, n_col)
            def _(k):
                row_copy(u // chips, k).start()

        @pl.when(last)
        def _():
            pair_copy(t).wait_recv()
            col_out[2 * t + 1] = col_out[2 * t + 1] + pair_in[t]

            @pl.when(t < chips - 1)
            def _():
                chip_copy(t).start()

    total = col_out[2 * chips - 1]
    for t in range(chips - 1):
        chip_copy(t).wait_recv()
        total = total + chip_in[t]
    col_share[...] = total[0:dim]
    for h in range(halves):
        row_total = row_sum[h, c]
        for k in range(1, n_col):
            row_copy(h, k).wait_recv()
            row_total = row_total + row_in[h, k]
        row_share[:, h * piece : (h + 1) * piece] = row_total[0:dim]

    @pl.loop(0, chips)
    def _(t):
        pair_copy(t).wait_send()

    @pl.loop(0, chips - 1)
    def _(t):
        chip_copy(t).wait_send()

    for h in range(halves):

        @pl.loop(1, n_col)
        def _(k):
            row_copy(h, k).wait_send()


def gradients(n_row, n_col, half_scale, table, rows, cols, gain, offset, row_part, col_part):
    f32 = jnp.float32
    bf16 = jnp.bfloat16
    dim, row_width = rows.shape[1:]
    col_width = cols.shape[2]
    dim_pad = round_up(dim, 16)
    depth = round_up(3 * dim_pad, 128)
    halves = 2 if row_width % 256 == 0 else 1
    piece = row_width // halves
    half_rows = n_col * piece
    tile_rows = n_col * row_width
    sub_cols = gain.shape[2]
    chips = n_row // 2
    smem = pl.BlockSpec(memory_space=pltpu.SMEM)
    vmem = pl.BlockSpec(memory_space=pltpu.VMEM)
    dma = pltpu.SemaphoreType.DMA
    return pl.pallas_call(
        functools.partial(gradient_kernel, n_row, n_col, dim, dim_pad, depth, half_scale),
        out_shape=(
            jax.ShapeDtypeStruct((dim, row_width), f32),
            jax.ShapeDtypeStruct((dim, col_width), f32),
        ),
        in_specs=[smem] + [vmem] * 6,
        out_specs=(vmem,) * 2,
        scratch_shapes=[
            pltpu.VMEM((tile_rows, sub_cols), f32),
            pltpu.VMEM(col_part.shape, f32),
            pltpu.VMEM((n_col,) + row_part.shape, f32),
            pltpu.VMEM((n_row,) + col_part.shape, f32),
            pltpu.VMEM((8, sub_cols), f32),
            pltpu.VMEM((n_col, 8, sub_cols), f32),
            pltpu.VMEM((dim_pad, row_width), f32),
            pltpu.VMEM((dim_pad, col_width), f32),
            pltpu.VMEM((halves, depth, half_rows), bf16),
            pltpu.VMEM((halves, half_rows, depth), bf16),
            pltpu.VMEM((depth, col_width), bf16),
            pltpu.VMEM((depth, col_width), bf16),
            pltpu.VMEM((half_rows, col_width), f32),
            pltpu.VMEM((half_rows, col_width), f32),
            pltpu.VMEM((half_rows, col_width), bf16),
            pltpu.VMEM((half_rows, col_width), bf16),
            pltpu.VMEM((halves, n_col, dim_pad, piece), f32),
            pltpu.VMEM((2 * chips, dim_pad, col_width), f32),
            pltpu.VMEM((chips, dim_pad, col_width), f32),
            pltpu.VMEM((max(chips - 1, 1), dim_pad, col_width), f32),
            pltpu.VMEM((halves, n_col, dim_pad, piece), f32),
            dma((chips,)), dma((chips,)), dma((chips,)), dma((chips,)),
            dma((halves * n_col,)), dma((halves * n_col,)),
            dma((n_col,)), dma((n_col,)), dma((n_row,)), dma((n_row,)), dma((n_col,)), dma((n_col,)),
        ],
        compiler_params=pltpu.CompilerParams(
            collective_id=1, has_side_effects=True, vmem_limit_bytes=VMEM_LIMIT
        ),
        name="gradients",
    )(table, rows, cols, gain, offset, row_part, col_part)


def per_device(blocks, plan, live, row_emb, col_emb, row_acc, col_acc):
    n_row = lax.axis_size("row")
    n_col = lax.axis_size("col")
    sub_rows, sub_cols = blocks.shape[5:]
    tile_rows = row_emb.shape[1] * n_col
    tile_cols = col_emb.shape[1] * n_row
    scale = 4.0 * float(tile_rows * n_row * tile_cols * n_col) ** (-0.25)
    arrived, rows, cols = exchange(n_row, n_col, blocks[0, 0], row_emb, col_emb)
    places = plan[0, 0]
    slot_ids = lax.broadcasted_iota(jnp.int32, places.shape, 2)
    alive = (slot_ids < live[0, 0][:, :, None]).astype(jnp.int32)
    gain, offset, table, row_part, col_part = merge(
        scale, places.reshape(-1), alive.reshape(-1), arrived.reshape(-1, sub_rows, sub_cols),
        tile_rows // sub_rows, tile_cols // sub_cols,
    )
    row_share, col_share = gradients(
        n_row, n_col, 0.5 * scale, table, rows, cols, gain, offset, row_part, col_part
    )
    new_row_acc = row_acc + row_share * row_share
    new_col_acc = col_acc + col_share * col_share
    new_row_emb = row_emb - LEARNING_RATE * row_share / jnp.sqrt(new_row_acc)
    new_col_emb = col_emb - LEARNING_RATE * col_share / jnp.sqrt(new_col_acc)
    return (new_row_emb, new_col_emb, new_row_acc, new_col_acc)


def solution(mesh):
    return jax.shard_map(
        per_device,
        mesh=mesh,
        in_specs=(
            P("row", "col", None, None, None, None, None),
            P("row", "col", None, None, None),
            P("row", "col", None, None),
            P(None, ("row", "col")),
            P(None, ("col", "row")),
            P(None, ("row", "col")),
            P(None, ("col", "row")),
        ),
        out_specs=(
            P(None, ("row", "col")),
            P(None, ("col", "row")),
            P(None, ("row", "col")),
            P(None, ("col", "row")),
        ),
        check_vma=False,
    )
```
